32 devices in a mesh: grp: 4 (over y, x), peer: 8 (over z, core).
Axes of the slice: x: 2, y: 2, z: 4, core: 2. Of those that a mesh axis runs over, the one named last changes fastest.
Arguments:
- embeddings: bfloat16 [16384, 768], P(('grp', 'peer')), may hold values from -6 to 6
- seed_labels: float32 [16384, 128], P(('grp', 'peer')), may hold values from -6 to 6
- cluster_ids: int32 [16384], P(('grp', 'peer')), may hold values from 0 to 63, as said below
- owner_map: int32 [64], replicated, may hold values from 0 to 31, as said below
- seed_flags: int32 [16384], P(('grp', 'peer')), may hold values 0 or 1
Outputs:
- refined: float32 [16384, 128], P(('grp', 'peer'))
The draws below stay inside these ranges and needn't reach their ends.
Inputs may be any that keep to these rules, and one draw needn't show every extreme that they name: `cluster_ids`: within each device's aligned block of 512 rows, at most 32 rows name clusters owned by any one device; one device owns clusters named by exactly 32 rows of every block. `owner_map`: every device owns exactly 2 clusters.
All inputs are finite; a program needn't handle non-finite values. No bound on the sum of `seed_flags` on one device may be relied on, other than what follows from the above.
Results may differ from the reference program's by a relative error of at most 0.0031.
Values may be sent and summed in bfloat16 or wider, within the bound.
A program may use at most 64 MiB of HBM per device.

```python
import math
import jax
import jax.numpy as jnp
from jax import lax

D = 768
LAB = 128
TOK_DEV = 512
CL_DEV = 2
STEPS = 3
TOKENS = 16384
CAP = 32
N_GRP = 4
N_PEER = 8


def routing_tables(key):
    base = jax.random.fold_in(key, 11)
    key_perm, key_busy, key_slots, key_shuffle, key_pick = jax.random.split(base, 5)
    device_count = N_GRP * N_PEER
    cluster_count = CL_DEV * device_count
    ranking = jax.random.permutation(key_perm, cluster_count).astype(jnp.int32)
    owner_map = (ranking // CL_DEV).astype(jnp.int32)
    owned = jnp.argsort(ranking).astype(jnp.int32).reshape(device_count, CL_DEV)
    busiest = jax.random.randint(key_busy, (), 0, device_count)
    slot_total = device_count * CAP
    slot_owner = jnp.arange(slot_total, dtype=jnp.int32) // CAP
    orders = jax.vmap(lambda one_key: jax.random.permutation(one_key, slot_total))(jax.random.split(key_slots, device_count)).astype(jnp.int32)
    priority = jnp.where(slot_owner[None, :] == busiest, jnp.arange(slot_total, dtype=jnp.int32)[None, :] - slot_total, orders)
    chosen = jnp.argsort(priority, axis=1)[:, :TOK_DEV]
    row_owner = slot_owner[chosen]
    shuffle = jax.vmap(lambda one_key: jax.random.permutation(one_key, TOK_DEV))(jax.random.split(key_shuffle, device_count)).astype(jnp.int32)
    row_owner = jnp.take_along_axis(row_owner, shuffle, axis=1)
    pick = jax.random.randint(key_pick, (device_count, TOK_DEV), 0, CL_DEV)
    cluster_ids = owned[row_owner, pick].reshape(-1).astype(jnp.int32)
    return (owner_map, cluster_ids)


def draw_owner_map(key, part):
    owner_map, cluster_ids = routing_tables(key)
    return owner_map


def draw_cluster_ids(key, part):
    owner_map, cluster_ids = routing_tables(key)
    return cluster_ids


def draw_embeddings(key, part):
    key_base = jax.random.fold_in(jax.random.fold_in(key, 23), 0)
    values = jax.random.truncated_normal(key_base, -6.0, 6.0, (TOKENS, D), jnp.float32)
    return values.astype(jnp.bfloat16)


def plant(values, stream_key, smallest, top_value):
    longest = values.shape.index(max(values.shape))
    spots = []
    for shift in (0, 1):
        where = [jax.random.randint(jax.random.fold_in(stream_key, axis), (), 0, length) for axis, length in enumerate(values.shape)]
        where[longest] = (where[longest] + shift) % values.shape[longest]
        spots.append(tuple(where))
    return values.at[spots[0]].set(smallest).at[spots[1]].set(top_value)


def block_levels(key, dims, cuts, least, high):
    level, own = 1.0, jax.random.fold_in(key, 6)
    for dim, parts in cuts:
        heights = jnp.exp(jax.random.uniform(jax.random.fold_in(own, dim), (parts,), jnp.float32, least / len(cuts), high / len(cuts)))
        level = level * jnp.repeat(heights, dims[dim] // parts).reshape([-1 if axis == dim else 1 for axis in range(len(dims))])
    return level


def bell_draw(own_key, dims, width, limit, cuts=(), kind=jnp.bfloat16):
    entries = width * jax.random.normal(own_key, dims, jnp.float32)
    if cuts:
        entries = entries * block_levels(own_key, dims, cuts, -0.22, 0.18)
    return jnp.clip(entries, -limit, limit).astype(kind)


def setup_inputs(seed: int = 0) -> dict:
    splits = jax.random.split(jax.random.key(seed), 6)
    embeddings = draw_embeddings(jax.random.fold_in(splits[5], 71), 0)
    seed_labels = bell_draw(splits[1], (TOKENS, LAB), 1.0, 6.0, ((0, 32),), jnp.float32)
    cluster_ids = draw_cluster_ids(jax.random.fold_in(splits[5], 71), 0)
    owner_map = draw_owner_map(jax.random.fold_in(splits[5], 71), 0)
    seed_flags = plant((jax.random.randint(splits[4], (TOKENS,), 0, 4) < 1).astype(jnp.int32), jax.random.fold_in(splits[4], 1), 0, 1)
    return {"embeddings": embeddings, "seed_labels": seed_labels, "cluster_ids": cluster_ids, "owner_map": owner_map, "seed_flags": seed_flags}


label_mix = 0.8
cross_penalty = 2.0

def affinity_rows(queries, keys, query_clusters, key_clusters, key_valid, offset):
    scale = 2.0 / math.sqrt(keys.shape[1])
    scores = lax.dot_general(queries, keys, (((1,), (1,)), ((), ())), preferred_element_type=jnp.float32) * scale
    query_pos = offset + jnp.arange(queries.shape[0], dtype=jnp.int32)
    key_pos = jnp.arange(keys.shape[0], dtype=jnp.int32)
    differ = query_clusters[:, None] != key_clusters[None, :]
    scores = jnp.where(differ, scores - cross_penalty, scores)
    scores = jnp.where(key_valid[None, :], scores, -jnp.inf)
    scores = jnp.where(query_pos[:, None] == key_pos[None, :], 0.0, scores)
    highest = lax.optimization_barrier(jnp.max(scores, axis=1, keepdims=True))
    weights = jnp.exp(scores - highest)
    return (weights / lax.optimization_barrier(jnp.sum(weights, axis=1, keepdims=True))).astype(jnp.bfloat16)

def propagate(group_emb, group_lab, group_clusters, group_seed, group_valid):
    slot_count = group_emb.shape[0]
    block = min(512, slot_count)
    pieces = []
    for offset in range(0, slot_count, block):
        pieces.append(affinity_rows(group_emb[offset:offset + block], group_emb, group_clusters[offset:offset + block], group_clusters, group_valid, offset))
    affinity = jnp.concatenate(pieces, axis=0)
    current = group_lab
    for sweep in range(STEPS):
        spread = jnp.dot(affinity, current.astype(jnp.bfloat16), preferred_element_type=jnp.float32)
        current = jnp.where(group_seed[:, None] > 0, group_lab, label_mix * spread + (1.0 - label_mix) * group_lab)
    return current

def reference(embeddings, seed_labels, cluster_ids, owner_map, seed_flags):
    total = embeddings.shape[0]
    device_count = N_GRP * N_PEER
    slot_count = 2 * TOK_DEV
    owner_of = owner_map[cluster_ids].astype(jnp.int32)
    order = jnp.argsort(owner_of, stable=True).astype(jnp.int32)
    counts = lax.optimization_barrier(jnp.sum((owner_of[None, :] == jnp.arange(device_count, dtype=jnp.int32)[:, None]).astype(jnp.int32), axis=1)).astype(jnp.int32)
    starts = (jnp.cumsum(counts) - counts).astype(jnp.int32)

    def one_owner(owner_index):
        position = jnp.arange(slot_count, dtype=jnp.int32)
        valid = position < counts[owner_index]
        index = order[jnp.minimum(starts[owner_index] + position, total - 1).astype(jnp.int32)]
        group_emb = jnp.where(valid[:, None], embeddings[index], jnp.zeros((), embeddings.dtype))
        group_lab = jnp.where(valid[:, None], seed_labels[index], jnp.zeros((), seed_labels.dtype))
        group_clusters = jnp.where(valid, cluster_ids[index], -1).astype(jnp.int32)
        group_seed = jnp.where(valid, seed_flags[index], 0).astype(jnp.int32)
        result = propagate(group_emb, group_lab, group_clusters, group_seed, valid)
        target = jnp.where(valid, index, total).astype(jnp.int32)
        return (result, target)
    results, targets = lax.map(one_owner, jnp.arange(device_count, dtype=jnp.int32))
    refined = jnp.zeros((total, seed_labels.shape[1]), seed_labels.dtype)
    return refined.at[targets.reshape(-1)].set(results.reshape(-1, seed_labels.shape[1]), mode='drop')
```

```python
import functools
import math

import jax
import jax.numpy as jnp
from jax import lax
from jax.experimental import pallas as pl
from jax.experimental.pallas import tpu as pltpu
from jax.sharding import PartitionSpec as P

STEPS = 3
label_mix = 0.8
cross_penalty = 2.0
MESH = pl.DeviceIdType.MESH
EMB, LABEL, INFO, BACK = range(4)
HALF = 64
NT = (((1,), (1,)), ((), ()))


def dot(a, b):
    return jnp.dot(a, b, preferred_element_type=jnp.float32)


def dot_nt(a, b):
    return lax.dot_general(a, b, NT, preferred_element_type=jnp.float32)


def iota(shape, dim):
    return lax.broadcasted_iota(jnp.int32, shape, dim)


def one_hot(mask):
    return jnp.where(mask, 1.0, 0.0).astype(jnp.bfloat16)


def kernel(
    n_grp, n_peer, cap,
    emb_ref, lab_ref, ids_ref, own_ref, flg_ref, out_ref,
    send_emb, send_lab, send_info, recv_emb, recv_lab, recv_info, send_back, recv_back,
    target_row, affinity, carried, send_sem, recv_sem,
):
    n = n_grp * n_peer
    my_grp, my_peer = lax.axis_index("grp"), lax.axis_index("peer")
    me = my_grp * n_peer + my_peer
    rows, slots = emb_ref.shape[0], n * cap
    chunk = n_peer * cap

    def block(device):
        return pl.ds(pl.multiple_of(device * cap, cap), cap)

    def part(kind, device):
        return {
            EMB: (send_emb.at[block(device), :], recv_emb),
            LABEL: (send_lab.at[block(device), :], recv_lab),
            BACK: (send_back.at[block(device), :], recv_back),
        }[kind]

    def copy(kind, device, source):
        if kind == INFO:
            src, dst = send_info.at[device], recv_info.at[source]
        else:
            src, buffer = part(kind, device)
            dst = buffer.at[block(source), :]
        return pltpu.make_async_remote_copy(
            src_ref=src,
            dst_ref=dst,
            send_sem=send_sem.at[kind, device],
            recv_sem=recv_sem.at[kind, source],
            device_id=(device // n_peer, lax.rem(device, n_peer)),
            device_id_type=MESH,
        )

    def others(body):
        def one(k, _):
            body(lax.rem(me + k, n))
            return 0

        lax.fori_loop(1, n, one, 0)

    barrier = pltpu.get_barrier_semaphore()
    others(
        lambda d: pl.semaphore_signal(
            barrier, inc=1, device_id=(d // n_peer, lax.rem(d, n_peer)), device_id_type=MESH
        )
    )

    ids = ids_ref[...].reshape(1, rows)
    flags = flg_ref[...].reshape(1, rows)
    clusters = own_ref.shape[0]
    owners = own_ref[...].reshape(1, clusters).astype(jnp.bfloat16)
    owners = jnp.broadcast_to(owners, (16, clusters))
    owner = dot(owners, one_hot(iota((clusters, rows), 0) == ids))[0:1, :].astype(jnp.int32)
    member = iota((n, rows), 0) == owner
    members = one_hot(member)
    running = dot(members, one_hot(iota((rows, rows), 0) <= iota((rows, rows), 1)))
    position = jnp.sum(jnp.where(member, running, 0.0), axis=0, keepdims=True).astype(jnp.int32) - 1
    target = owner * cap + position
    target_row[...] = target
    lane = iota((128, rows), 0)
    entry = jnp.where(
        lane < HALF,
        jnp.where(lane == position, (ids + 1).astype(jnp.float32), 0.0),
        jnp.where(lane - HALF == position, flags.astype(jnp.float32), 0.0),
    ).astype(jnp.bfloat16)
    send_info[...] = dot_nt(members, entry).reshape(n, 1, 128)
    recv_info[me] = send_info[me]

    pl.semaphore_wait(barrier, n - 1)

    def send_chunk(j, _):
        g = lax.rem(my_grp + j, n_grp)
        start = pl.multiple_of(g * chunk, chunk)
        pick = one_hot(iota((chunk, rows), 0) + start == target_row[...])
        send_emb[pl.ds(start, chunk), :] = dot(pick, emb_ref[...]).astype(jnp.bfloat16)

        def one(k, _):
            d = g * n_peer + lax.rem(my_peer + k, n_peer)

            @pl.when(d != me)
            def _():
                copy(EMB, d, me).start()

            return 0

        lax.fori_loop(0, n_peer, one, 0)
        send_lab[pl.ds(start, chunk), :] = dot(pick, lab_ref[...].astype(jnp.bfloat16)).astype(jnp.bfloat16)
        return 0

    lax.fori_loop(1, n_grp + 1, send_chunk, 0)

    def send_small(d):
        copy(INFO, d, me).start()
        copy(LABEL, d, me).start()

    others(send_small)
    recv_emb[block(me), :] = send_emb[block(me), :]
    recv_lab[block(me), :] = send_lab[block(me), :]

    others(lambda s: copy(EMB, s, s).wait_recv())
    others(lambda s: copy(INFO, s, s).wait_recv())

    info = recv_info[...].reshape(n, 128).astype(jnp.bfloat16)
    slot = iota((slots, 128), 0)
    place = iota((slots, 128), 1)
    spread_info = dot(one_hot(iota((slots, n), 0) // cap == iota((slots, n), 1)), info)
    here = slot - slot // cap * cap
    cluster_col = jnp.sum(jnp.where(place == here, spread_info, 0.0), axis=1, keepdims=True)
    seed_col = jnp.sum(jnp.where(place == here + HALF, spread_info, 0.0), axis=1, keepdims=True)
    along = iota((128, slots), 1)
    wide = dot(info, one_hot(iota((128, slots), 0) == along - along // cap * cap))
    cluster_row = jnp.sum(
        jnp.where(iota((n, slots), 0) == iota((n, slots), 1) // cap, wide, 0.0), axis=0, keepdims=True
    )
    scale = 2.0 / math.sqrt(emb_ref.shape[1])
    for offset in range(0, slots, chunk):
        score = dot_nt(recv_emb[pl.ds(offset, chunk), :], recv_emb[...]) * scale
        score = jnp.where(cluster_col[offset : offset + chunk] != cluster_row, score - cross_penalty, score)
        score = jnp.where(cluster_row > 0.5, score, -1e30)
        score = jnp.where(iota(score.shape, 0) + offset == iota(score.shape, 1), 0.0, score)
        weight = jnp.exp(score - jnp.max(score, axis=1, keepdims=True))
        total = jnp.sum(weight, axis=1, keepdims=True)
        affinity[pl.ds(offset, chunk), :] = (weight * (1.0 / total)).astype(jnp.bfloat16)

    others(lambda s: copy(LABEL, s, s).wait_recv())
    given = recv_lab[...].astype(jnp.float32)
    fixed = seed_col > 0.5
    carried[...] = recv_lab[...]
    for sweep in range(STEPS - 1):
        spread = dot(affinity[...], carried[...])
        current = jnp.where(fixed, given, label_mix * spread + (1.0 - label_mix) * given)
        carried[...] = current.astype(jnp.bfloat16)

    def back_chunk(j, _):
        g = lax.rem(my_grp + j, n_grp)
        piece = pl.ds(pl.multiple_of(g * chunk, chunk), chunk)
        send_back[piece, :] = dot(affinity[piece, :], carried[...]).astype(jnp.bfloat16)

        def one(k, _):
            d = g * n_peer + lax.rem(my_peer + k, n_peer)

            @pl.when(d != me)
            def _():
                copy(BACK, d, me).start()

            return 0

        lax.fori_loop(0, n_peer, one, 0)
        return 0

    lax.fori_loop(1, n_grp + 1, back_chunk, 0)
    recv_back[block(me), :] = send_back[block(me), :]

    side = jnp.concatenate([target_row[...], flags, jnp.zeros((6, rows), jnp.int32)], axis=0)
    side = jnp.transpose(side.astype(jnp.float32)).astype(jnp.int32)
    home = one_hot(iota((rows, slots), 1) == side[:, 0:1])
    kept = side[:, 1:2] > 0
    others(lambda s: copy(BACK, s, s).wait_recv())
    spread = dot(home, recv_back[...])
    seed = lab_ref[...]
    out_ref[...] = jnp.where(kept, seed, label_mix * spread + (1.0 - label_mix) * seed)

    def sent(d):
        for kind in (EMB, LABEL, INFO, BACK):
            copy(kind, d, me).wait_send()

    others(sent)


def solution(mesh):
    n_grp, n_peer = mesh.shape["grp"], mesh.shape["peer"]
    n = n_grp * n_peer

    def step(embeddings, seed_labels, cluster_ids, owner_map, seed_flags):
        rows, depth = embeddings.shape
        width = seed_labels.shape[1]
        cap = max(2 * rows // n, 16)
        slots = n * cap
        buffers = [
            pltpu.VMEM((slots, depth), jnp.bfloat16),
            pltpu.VMEM((slots, width), jnp.bfloat16),
            pltpu.VMEM((n, 1, 128), jnp.float32),
        ]
        return pl.pallas_call(
            functools.partial(kernel, n_grp, n_peer, cap),
            out_shape=jax.ShapeDtypeStruct((rows, width), jnp.float32),
            in_specs=[pl.BlockSpec(memory_space=pltpu.VMEM)] * 5,
            out_specs=pl.BlockSpec(memory_space=pltpu.VMEM),
            scratch_shapes=[
                *buffers,
                *buffers,
                pltpu.VMEM((slots, width), jnp.bfloat16),
                pltpu.VMEM((slots, width), jnp.bfloat16),
                pltpu.VMEM((1, rows), jnp.int32),
                pltpu.VMEM((slots, slots), jnp.bfloat16),
                pltpu.VMEM((slots, width), jnp.bfloat16),
                pltpu.SemaphoreType.DMA((4, n)),
                pltpu.SemaphoreType.DMA((4, n)),
            ],
            compiler_params=pltpu.CompilerParams(
                collective_id=0, has_side_effects=True, vmem_limit_bytes=56 * 1024 * 1024
            ),
        )(embeddings, seed_labels, cluster_ids, owner_map, seed_flags)

    rows = P(("grp", "peer"))
    return jax.shard_map(
        step,
        mesh=mesh,
        in_specs=(P(("grp", "peer"), None), P(("grp", "peer"), None), rows, P(), rows),
        out_specs=P(("grp", "peer"), None),
        check_vma=False,
    )
```

```python
import functools
import math

import jax
import jax.numpy as jnp
from jax import lax
from jax.experimental import pallas as pl
from jax.experimental.pallas import tpu as pltpu
from jax.sharding import PartitionSpec as P

STEPS = 3
label_mix = 0.8
cross_penalty = 2.0
MESH = pl.DeviceIdType.MESH
EMB, LABEL, INFO, BACK = range(4)
HALF = 64
NT = (((1,), (1,)), ((), ()))


def dot(a, b):
    return jnp.dot(a, b, preferred_element_type=jnp.float32)


def dot_nt(a, b):
    return lax.dot_general(a, b, NT, preferred_element_type=jnp.float32)


def iota(shape, dim):
    return lax.broadcasted_iota(jnp.int32, shape, dim)


def one_hot(mask):
    return jnp.where(mask, 1.0, 0.0).astype(jnp.bfloat16)


def kernel(
    n_grp, n_peer, cap,
    emb_ref, lab_ref, ids_ref, own_ref, flg_ref, out_ref,
    send_emb, send_lab, send_info, recv_emb, recv_lab, recv_info, send_back, recv_back,
    target_row, home, affinity, carried, send_sem, recv_sem,
):
    n = n_grp * n_peer
    my_grp, my_peer = lax.axis_index("grp"), lax.axis_index("peer")
    me = my_grp * n_peer + my_peer
    rows, slots = emb_ref.shape[0], n * cap
    chunk = n_peer * cap

    def block(device):
        return pl.ds(pl.multiple_of(device * cap, cap), cap)

    def part(kind, device):
        return {
            EMB: (send_emb.at[block(device), :], recv_emb),
            LABEL: (send_lab.at[block(device), :], recv_lab),
            BACK: (send_back.at[block(device), :], recv_back),
        }[kind]

    def copy(kind, device, source):
        if kind == INFO:
            src, dst = send_info.at[device], recv_info.at[source]
        else:
            src, buffer = part(kind, device)
            dst = buffer.at[block(source), :]
        return pltpu.make_async_remote_copy(
            src_ref=src,
            dst_ref=dst,
            send_sem=send_sem.at[kind],
            recv_sem=recv_sem.at[kind],
            device_id=(lax.div(device, n_peer), lax.rem(device, n_peer)),
            device_id_type=MESH,
        )

    def whole(kind):
        source, landing = {
            EMB: (send_emb, recv_emb),
            LABEL: (send_lab, recv_lab),
            INFO: (send_info, recv_info),
            BACK: (send_back, recv_back),
        }[kind]
        part = pl.ds(0, (n - 1) * (1 if kind == INFO else cap))
        right = lax.rem(me + 1, n)
        return pltpu.make_async_remote_copy(
            src_ref=source.at[part],
            dst_ref=landing.at[part],
            send_sem=send_sem.at[kind],
            recv_sem=recv_sem.at[kind],
            device_id=(lax.div(right, n_peer), lax.rem(right, n_peer)),
            device_id_type=MESH,
        )

    def others(body):
        for k in range(1, n):
            body(lax.rem(me + k, n))

    def members_of(j, body):
        g = lax.rem(my_grp + j, n_grp)
        for k in range(1 if j == n_grp else 0, n_peer):
            body(g * n_peer + lax.rem(my_peer + k, n_peer))

    barrier = pltpu.get_barrier_semaphore()
    others(
        lambda d: pl.semaphore_signal(
            barrier, inc=1, device_id=(lax.div(d, n_peer), lax.rem(d, n_peer)), device_id_type=MESH
        )
    )

    ids = ids_ref[...].reshape(1, rows)
    flags = flg_ref[...].reshape(1, rows)
    clusters = own_ref.shape[0]
    owners = own_ref[...].reshape(1, clusters).astype(jnp.bfloat16)
    owners = jnp.broadcast_to(owners, (16, clusters))
    owner = dot(owners, one_hot(iota((clusters, rows), 0) == ids))[0:1, :].astype(jnp.int32)
    member = iota((n, rows), 0) == owner
    members = one_hot(member)
    running = dot(members, one_hot(iota((rows, rows), 0) <= iota((rows, rows), 1)))
    position = jnp.sum(jnp.where(member, running, 0.0), axis=0, keepdims=True).astype(jnp.int32) - 1
    target = owner * cap + position
    target_row[...] = target
    lane = iota((128, rows), 0)
    entry = jnp.where(
        lane < HALF,
        jnp.where(lane == position, (ids + 1).astype(jnp.float32), 0.0),
        jnp.where(lane - HALF == position, flags.astype(jnp.float32), 0.0),
    ).astype(jnp.bfloat16)
    send_info[...] = dot_nt(members, entry).reshape(n, 1, 128)
    recv_info[me] = send_info[me]

    for j in range(1, n_grp + 1):
        g = lax.rem(my_grp + j, n_grp)
        start = pl.multiple_of(g * chunk, chunk)
        pick = one_hot(iota((chunk, rows), 0) + start == target_row[...])
        send_emb[pl.ds(start, chunk), :] = dot(pick, emb_ref[...]).astype(jnp.bfloat16)
        if j == 1:
            pl.semaphore_wait(barrier, n - 1)
        members_of(j, lambda d: copy(EMB, d, me).start())
        members_of(j, lambda d: copy(INFO, d, me).start())
        send_lab[pl.ds(start, chunk), :] = dot(pick, lab_ref[...].astype(jnp.bfloat16)).astype(jnp.bfloat16)

    others(lambda d: copy(LABEL, d, me).start())
    recv_emb[block(me), :] = send_emb[block(me), :]
    recv_lab[block(me), :] = send_lab[block(me), :]

    side = jnp.concatenate([target_row[...], flags, jnp.zeros((6, rows), jnp.int32)], axis=0)
    side = jnp.transpose(side.astype(jnp.float32)).astype(jnp.int32)
    home[...] = one_hot(iota((rows, slots), 1) == side[:, 0:1])
    kept = side[:, 1:2] > 0

    whole(INFO).wait_recv()
    info = recv_info[...].reshape(n, 128).astype(jnp.bfloat16)
    slot = iota((slots, 128), 0)
    place = iota((slots, 128), 1)
    spread_info = dot(one_hot(iota((slots, n), 0) // cap == iota((slots, n), 1)), info)
    here = slot - slot // cap * cap
    cluster_col = jnp.sum(jnp.where(place == here, spread_info, 0.0), axis=1, keepdims=True)
    seed_col = jnp.sum(jnp.where(place == here + HALF, spread_info, 0.0), axis=1, keepdims=True)
    along = iota((128, slots), 1)
    wide = dot(info, one_hot(iota((128, slots), 0) == along - along // cap * cap))
    cluster_row = jnp.sum(
        jnp.where(iota((n, slots), 0) == iota((n, slots), 1) // cap, wide, 0.0), axis=0, keepdims=True
    )
    whole(EMB).wait_recv()
    scale = 2.0 / math.sqrt(emb_ref.shape[1])
    for offset in range(0, slots, chunk):
        score = dot_nt(recv_emb[pl.ds(offset, chunk), :], recv_emb[...]) * scale
        score = jnp.where(cluster_col[offset : offset + chunk] != cluster_row, score - cross_penalty, score)
        score = jnp.where(cluster_row > 0.5, score, -1e30)
        score = jnp.where(iota(score.shape, 0) + offset == iota(score.shape, 1), 0.0, score)
        weight = jnp.exp(score - jnp.max(score, axis=1, keepdims=True))
        total = jnp.sum(weight, axis=1, keepdims=True)
        affinity[pl.ds(offset, chunk), :] = (weight * (1.0 / total)).astype(jnp.bfloat16)

    whole(LABEL).wait_recv()
    given = recv_lab[...].astype(jnp.float32)
    fixed = seed_col > 0.5
    carried[...] = recv_lab[...]
    for sweep in range(STEPS - 1):
        spread = dot(affinity[...], carried[...])
        current = jnp.where(fixed, given, label_mix * spread + (1.0 - label_mix) * given)
        carried[...] = current.astype(jnp.bfloat16)

    for j in range(1, n_grp + 1):
        g = lax.rem(my_grp + j, n_grp)
        piece = pl.ds(pl.multiple_of(g * chunk, chunk), chunk)
        send_back[piece, :] = dot(affinity[piece, :], carried[...]).astype(jnp.bfloat16)
        members_of(j, lambda d: copy(BACK, d, me).start())
    recv_back[block(me), :] = send_back[block(me), :]

    whole(BACK).wait_recv()
    spread = dot(home[...], recv_back[...])
    seed = lab_ref[...]
    out_ref[...] = jnp.where(kept, seed, label_mix * spread + (1.0 - label_mix) * seed)

    for kind in (EMB, LABEL, INFO, BACK):
        whole(kind).wait_send()


def solution(mesh):
    n_grp, n_peer = mesh.shape["grp"], mesh.shape["peer"]
    n = n_grp * n_peer

    def step(embeddings, seed_labels, cluster_ids, owner_map, seed_flags):
        rows, depth = embeddings.shape
        width = seed_labels.shape[1]
        cap = max(2 * rows // n, 16)
        slots = n * cap
        buffers = [
            pltpu.VMEM((slots, depth), jnp.bfloat16),
            pltpu.VMEM((slots, width), jnp.bfloat16),
            pltpu.VMEM((n, 1, 128), jnp.float32),
        ]
        return pl.pallas_call(
            functools.partial(kernel, n_grp, n_peer, cap),
            out_shape=jax.ShapeDtypeStruct((rows, width), jnp.float32),
            in_specs=[pl.BlockSpec(memory_space=pltpu.VMEM)] * 5,
            out_specs=pl.BlockSpec(memory_space=pltpu.VMEM),
            scratch_shapes=[
                *buffers,
                *buffers,
                pltpu.VMEM((slots, width), jnp.bfloat16),
                pltpu.VMEM((slots, width), jnp.bfloat16),
                pltpu.VMEM((1, rows), jnp.int32),
                pltpu.VMEM((rows, slots), jnp.bfloat16),
                pltpu.VMEM((slots, slots), jnp.bfloat16),
                pltpu.VMEM((slots, width), jnp.bfloat16),
                pltpu.SemaphoreType.DMA((4,)),
                pltpu.SemaphoreType.DMA((4,)),
            ],
            compiler_params=pltpu.CompilerParams(
                collective_id=0, has_side_effects=True, vmem_limit_bytes=56 * 1024 * 1024
            ),
        )(embeddings, seed_labels, cluster_ids, owner_map, seed_flags)

    rows = P(("grp", "peer"))
    return jax.shard_map(
        step,
        mesh=mesh,
        in_specs=(P(("grp", "peer"), None), P(("grp", "peer"), None), rows, P(), rows),
        out_specs=P(("grp", "peer"), None),
        check_vma=False,
    )
```

```python
import functools
import math

import jax
import jax.numpy as jnp
from jax import lax
from jax.experimental import pallas as pl
from jax.experimental.pallas import tpu as pltpu
from jax.sharding import PartitionSpec as P

STEPS = 3
label_mix = 0.8
cross_penalty = 2.0
MESH = pl.DeviceIdType.MESH
EMB, LABEL, INFO, BACK = range(4)
HALF = 64
NT = (((1,), (1,)), ((), ()))


def dot(a, b):
    return jnp.dot(a, b, preferred_element_type=jnp.float32)


def dot_nt(a, b):
    return lax.dot_general(a, b, NT, preferred_element_type=jnp.float32)


def iota(shape, dim):
    return lax.broadcasted_iota(jnp.int32, shape, dim)


def one_hot(mask):
    return jnp.where(mask, 1.0, 0.0).astype(jnp.bfloat16)


def kernel(
    n_grp, n_peer, cap,
    emb_ref, lab_ref, ids_ref, own_ref, flg_ref, out_ref,
    send_emb, send_lab, send_info, recv_emb, recv_lab, recv_info, send_back, recv_back,
    target_row, home, affinity, carried, send_sem, recv_sem,
):
    n = n_grp * n_peer
    my_grp, my_peer = lax.axis_index("grp"), lax.axis_index("peer")
    me = my_grp * n_peer + my_peer
    rows, slots = emb_ref.shape[0], n * cap
    chunk = n_peer * cap

    def block(device):
        return pl.ds(pl.multiple_of(device * cap, cap), cap)

    def part(kind, device):
        return {
            EMB: (send_emb.at[block(device), :], recv_emb),
            LABEL: (send_lab.at[block(device), :], recv_lab),
            BACK: (send_back.at[block(device), :], recv_back),
        }[kind]

    def copy(kind, device, source):
        if kind == INFO:
            src, dst = send_info.at[device], recv_info.at[source]
        else:
            src, buffer = part(kind, device)
            dst = buffer.at[block(source), :]
        return pltpu.make_async_remote_copy(
            src_ref=src,
            dst_ref=dst,
            send_sem=send_sem.at[kind],
            recv_sem=recv_sem.at[kind],
            device_id=(lax.div(device, n_peer), lax.rem(device, n_peer)),
            device_id_type=MESH,
        )

    def whole(kind):
        source, landing = {
            EMB: (send_emb, recv_emb),
            LABEL: (send_lab, recv_lab),
            INFO: (send_info, recv_info),
            BACK: (send_back, recv_back),
        }[kind]
        part = pl.ds(0, (n - 1) * (1 if kind == INFO else cap))
        right = lax.rem(me + 1, n)
        return pltpu.make_async_remote_copy(
            src_ref=source.at[part],
            dst_ref=landing.at[part],
            send_sem=send_sem.at[kind],
            recv_sem=recv_sem.at[kind],
            device_id=(lax.div(right, n_peer), lax.rem(right, n_peer)),
            device_id_type=MESH,
        )

    def others(body):
        for k in range(1, n):
            body(lax.rem(me + k, n))

    def members_of(j, body):
        g = lax.rem(my_grp + j, n_grp)
        far = n_peer // 2
        for k in sorted(range(1 if j == n_grp else 0, n_peer), key=lambda k: abs(k - far)):
            body(g * n_peer + lax.rem(my_peer + k, n_peer))

    barrier = pltpu.get_barrier_semaphore()
    others(
        lambda d: pl.semaphore_signal(
            barrier, inc=1, device_id=(lax.div(d, n_peer), lax.rem(d, n_peer)), device_id_type=MESH
        )
    )

    ids = ids_ref[...].reshape(1, rows)
    flags = flg_ref[...].reshape(1, rows)
    clusters = own_ref.shape[0]
    owners = own_ref[...].reshape(1, clusters).astype(jnp.bfloat16)
    owners = jnp.broadcast_to(owners, (16, clusters))
    owner = dot(owners, one_hot(iota((clusters, rows), 0) == ids))[0:1, :].astype(jnp.int32)
    member = iota((n, rows), 0) == owner
    members = one_hot(member)
    running = dot(members, one_hot(iota((rows, rows), 0) <= iota((rows, rows), 1)))
    position = jnp.sum(jnp.where(member, running, 0.0), axis=0, keepdims=True).astype(jnp.int32) - 1
    target = owner * cap + position
    target_row[...] = target

    for j in range(1, n_grp + 1):
        g = lax.rem(my_grp + j, n_grp)
        start = pl.multiple_of(g * chunk, chunk)
        pick = one_hot(iota((chunk, rows), 0) + start == target_row[...])
        send_emb[pl.ds(start, chunk), :] = dot(pick, emb_ref[...]).astype(jnp.bfloat16)
        if j == 1:
            pl.semaphore_wait(barrier, n - 1)
        members_of(j, lambda d: copy(EMB, d, me).start())
        if j == 1:
            lane = iota((128, rows), 0)
            entry = jnp.where(
                lane < HALF,
                jnp.where(lane == position, (ids + 1).astype(jnp.float32), 0.0),
                jnp.where(lane - HALF == position, flags.astype(jnp.float32), 0.0),
            ).astype(jnp.bfloat16)
            send_info[...] = dot_nt(members, entry).reshape(n, 1, 128)
            recv_info[me] = send_info[me]
            others(lambda d: copy(INFO, d, me).start())
        send_lab[pl.ds(start, chunk), :] = dot(pick, lab_ref[...].astype(jnp.bfloat16)).astype(jnp.bfloat16)

    others(lambda d: copy(LABEL, d, me).start())
    recv_emb[block(me), :] = send_emb[block(me), :]
    recv_lab[block(me), :] = send_lab[block(me), :]

    side = jnp.concatenate([target_row[...], flags, jnp.zeros((6, rows), jnp.int32)], axis=0)
    side = jnp.transpose(side.astype(jnp.float32)).astype(jnp.int32)
    home[...] = one_hot(iota((rows, slots), 1) == side[:, 0:1])
    kept = side[:, 1:2] > 0

    whole(INFO).wait_recv()
    info = recv_info[...].reshape(n, 128).astype(jnp.bfloat16)
    slot = iota((slots, 128), 0)
    place = iota((slots, 128), 1)
    spread_info = dot(one_hot(iota((slots, n), 0) // cap == iota((slots, n), 1)), info)
    here = slot - slot // cap * cap
    cluster_col = jnp.sum(jnp.where(place == here, spread_info, 0.0), axis=1, keepdims=True)
    seed_col = jnp.sum(jnp.where(place == here + HALF, spread_info, 0.0), axis=1, keepdims=True)
    along = iota((128, slots), 1)
    wide = dot(info, one_hot(iota((128, slots), 0) == along - along // cap * cap))
    cluster_row = jnp.sum(
        jnp.where(iota((n, slots), 0) == iota((n, slots), 1) // cap, wide, 0.0), axis=0, keepdims=True
    )
    whole(EMB).wait_recv()
    scale = 2.0 / math.sqrt(emb_ref.shape[1])
    for offset in range(0, slots, chunk):
        score = dot_nt(recv_emb[pl.ds(offset, chunk), :], recv_emb[...]) * scale
        score = jnp.where(cluster_col[offset : offset + chunk] != cluster_row, score - cross_penalty, score)
        score = jnp.where(cluster_row > 0.5, score, -1e30)
        score = jnp.where(iota(score.shape, 0) + offset == iota(score.shape, 1), 0.0, score)
        weight = jnp.exp(score - jnp.max(score, axis=1, keepdims=True))
        total = jnp.sum(weight, axis=1, keepdims=True)
        affinity[pl.ds(offset, chunk), :] = (weight * (1.0 / total)).astype(jnp.bfloat16)

    whole(LABEL).wait_recv()
    given = recv_lab[...].astype(jnp.float32)
    fixed = seed_col > 0.5
    carried[...] = recv_lab[...]
    for sweep in range(STEPS - 1):
        spread = dot(affinity[...], carried[...])
        current = jnp.where(fixed, given, label_mix * spread + (1.0 - label_mix) * given)
        carried[...] = current.astype(jnp.bfloat16)

    for j in range(1, n_grp + 1):
        g = lax.rem(my_grp + j, n_grp)
        piece = pl.ds(pl.multiple_of(g * chunk, chunk), chunk)
        send_back[piece, :] = dot(affinity[piece, :], carried[...]).astype(jnp.bfloat16)
        members_of(j, lambda d: copy(BACK, d, me).start())
    recv_back[block(me), :] = send_back[block(me), :]

    whole(BACK).wait_recv()
    spread = dot(home[...], recv_back[...])
    seed = lab_ref[...]
    out_ref[...] = jnp.where(kept, seed, label_mix * spread + (1.0 - label_mix) * seed)

    for kind in (EMB, LABEL, INFO, BACK):
        whole(kind).wait_send()


def solution(mesh):
    n_grp, n_peer = mesh.shape["grp"], mesh.shape["peer"]
    n = n_grp * n_peer

    def step(embeddings, seed_labels, cluster_ids, owner_map, seed_flags):
        rows, depth = embeddings.shape
        width = seed_labels.shape[1]
        cap = max(2 * rows // n, 16)
        slots = n * cap
        buffers = [
            pltpu.VMEM((slots, depth), jnp.bfloat16),
            pltpu.VMEM((slots, width), jnp.bfloat16),
            pltpu.VMEM((n, 1, 128), jnp.float32),
        ]
        return pl.pallas_call(
            functools.partial(kernel, n_grp, n_peer, cap),
            out_shape=jax.ShapeDtypeStruct((rows, width), jnp.float32),
            in_specs=[pl.BlockSpec(memory_space=pltpu.VMEM)] * 5,
            out_specs=pl.BlockSpec(memory_space=pltpu.VMEM),
            scratch_shapes=[
                *buffers,
                *buffers,
                pltpu.VMEM((slots, width), jnp.bfloat16),
                pltpu.VMEM((slots, width), jnp.bfloat16),
                pltpu.VMEM((1, rows), jnp.int32),
                pltpu.VMEM((rows, slots), jnp.bfloat16),
                pltpu.VMEM((slots, slots), jnp.bfloat16),
                pltpu.VMEM((slots, width), jnp.bfloat16),
                pltpu.SemaphoreType.DMA((4,)),
                pltpu.SemaphoreType.DMA((4,)),
            ],
            compiler_params=pltpu.CompilerParams(
                collective_id=0, has_side_effects=True, vmem_limit_bytes=56 * 1024 * 1024
            ),
        )(embeddings, seed_labels, cluster_ids, owner_map, seed_flags)

    rows = P(("grp", "peer"))
    return jax.shard_map(
        step,
        mesh=mesh,
        in_specs=(P(("grp", "peer"), None), P(("grp", "peer"), None), rows, P(), rows),
        out_specs=P(("grp", "peer"), None),
        check_vma=False,
    )
```

```python
import functools
import math

import jax
import jax.numpy as jnp
from jax import lax
from jax.experimental import pallas as pl
from jax.experimental.pallas import tpu as pltpu
from jax.sharding import PartitionSpec as P

STEPS = 3
label_mix = 0.8
cross_penalty = 2.0
MESH = pl.DeviceIdType.MESH
EMB, LABEL, INFO, BACK = range(4)
HALF = 64
NT = (((1,), (1,)), ((), ()))


def dot(a, b):
    return jnp.dot(a, b, preferred_element_type=jnp.float32)


def dot_nt(a, b):
    return lax.dot_general(a, b, NT, preferred_element_type=jnp.float32)


def iota(shape, dim):
    return lax.broadcasted_iota(jnp.int32, shape, dim)


def one_hot(mask):
    return jnp.where(mask, 1.0, 0.0).astype(jnp.bfloat16)


def kernel(
    n_grp, n_peer, cap,
    emb_ref, lab_ref, ids_ref, own_ref, flg_ref, out_ref,
    send_emb, send_lab, send_info, recv_emb, recv_lab, recv_info, send_back, recv_back,
    target_row, home, affinity, carried, send_sem, recv_sem,
):
    n = n_grp * n_peer
    my_grp, my_peer = lax.axis_index("grp"), lax.axis_index("peer")
    me = my_grp * n_peer + my_peer
    rows, slots = emb_ref.shape[0], n * cap
    chunk = n_peer * cap

    def block(device):
        return pl.ds(pl.multiple_of(device * cap, cap), cap)

    def part(kind, device):
        return {
            EMB: (send_emb.at[block(device), :], recv_emb),
            LABEL: (send_lab.at[block(device), :], recv_lab),
            BACK: (send_back.at[block(device), :], recv_back),
        }[kind]

    def copy(kind, device, source):
        if kind == INFO:
            src, dst = send_info.at[device], recv_info.at[source]
        else:
            src, buffer = part(kind, device)
            dst = buffer.at[block(source), :]
        return pltpu.make_async_remote_copy(
            src_ref=src,
            dst_ref=dst,
            send_sem=send_sem.at[kind],
            recv_sem=recv_sem.at[kind],
            device_id=(lax.div(device, n_peer), lax.rem(device, n_peer)),
            device_id_type=MESH,
        )

    def whole(kind):
        source, landing = {
            EMB: (send_emb, recv_emb),
            LABEL: (send_lab, recv_lab),
            INFO: (send_info, recv_info),
            BACK: (send_back, recv_back),
        }[kind]
        part = pl.ds(0, (n - 1) * (1 if kind == INFO else cap))
        right = lax.rem(me + 1, n)
        return pltpu.make_async_remote_copy(
            src_ref=source.at[part],
            dst_ref=landing.at[part],
            send_sem=send_sem.at[kind],
            recv_sem=recv_sem.at[kind],
            device_id=(lax.div(right, n_peer), lax.rem(right, n_peer)),
            device_id_type=MESH,
        )

    def others(body):
        for k in range(1, n):
            body(lax.rem(me + k, n))

    def members_of(j, body):
        g = lax.rem(my_grp + j, n_grp)
        half = n_peer // 2
        side, low = lax.div(my_peer, half), lax.rem(my_peer, half)
        for k in range(half):
            body(g * n_peer + (1 - side) * half + lax.rem(low + k, half))
        for k in range(1 if j == n_grp else 0, half):
            body(g * n_peer + side * half + lax.rem(low + k, half))

    barrier = pltpu.get_barrier_semaphore()
    others(
        lambda d: pl.semaphore_signal(
            barrier, inc=1, device_id=(lax.div(d, n_peer), lax.rem(d, n_peer)), device_id_type=MESH
        )
    )

    ids = ids_ref[...].reshape(1, rows)
    flags = flg_ref[...].reshape(1, rows)
    clusters = own_ref.shape[0]
    owners = own_ref[...].reshape(1, clusters).astype(jnp.bfloat16)
    owners = jnp.broadcast_to(owners, (16, clusters))
    owner = dot(owners, one_hot(iota((clusters, rows), 0) == ids))[0:1, :].astype(jnp.int32)
    member = iota((n, rows), 0) == owner
    members = one_hot(member)
    running = dot(members, one_hot(iota((rows, rows), 0) <= iota((rows, rows), 1)))
    position = jnp.sum(jnp.where(member, running, 0.0), axis=0, keepdims=True).astype(jnp.int32) - 1
    target = owner * cap + position
    target_row[...] = target

    for j in range(1, n_grp + 1):
        g = lax.rem(my_grp + j, n_grp)
        start = pl.multiple_of(g * chunk, chunk)
        pick = one_hot(iota((chunk, rows), 0) + start == target_row[...])
        send_emb[pl.ds(start, chunk), :] = dot(pick, emb_ref[...]).astype(jnp.bfloat16)
        if j == 1:
            pl.semaphore_wait(barrier, n - 1)
        members_of(j, lambda d: copy(EMB, d, me).start())
        if j == 1:
            lane = iota((128, rows), 0)
            entry = jnp.where(
                lane < HALF,
                jnp.where(lane == position, (ids + 1).astype(jnp.float32), 0.0),
                jnp.where(lane - HALF == position, flags.astype(jnp.float32), 0.0),
            ).astype(jnp.bfloat16)
            send_info[...] = dot_nt(members, entry).reshape(n, 1, 128)
            recv_info[me] = send_info[me]
            others(lambda d: copy(INFO, d, me).start())
        send_lab[pl.ds(start, chunk), :] = dot(pick, lab_ref[...].astype(jnp.bfloat16)).astype(jnp.bfloat16)

    others(lambda d: copy(LABEL, d, me).start())
    recv_emb[block(me), :] = send_emb[block(me), :]
    recv_lab[block(me), :] = send_lab[block(me), :]

    side = jnp.concatenate([target_row[...], flags, jnp.zeros((6, rows), jnp.int32)], axis=0)
    side = jnp.transpose(side.astype(jnp.float32)).astype(jnp.int32)
    home[...] = one_hot(iota((rows, slots), 1) == side[:, 0:1])
    kept = side[:, 1:2] > 0

    whole(INFO).wait_recv()
    info = recv_info[...].reshape(n, 128).astype(jnp.bfloat16)
    slot = iota((slots, 128), 0)
    place = iota((slots, 128), 1)
    spread_info = dot(one_hot(iota((slots, n), 0) // cap == iota((slots, n), 1)), info)
    here = slot - slot // cap * cap
    cluster_col = jnp.sum(jnp.where(place == here, spread_info, 0.0), axis=1, keepdims=True)
    seed_col = jnp.sum(jnp.where(place == here + HALF, spread_info, 0.0), axis=1, keepdims=True)
    along = iota((128, slots), 1)
    wide = dot(info, one_hot(iota((128, slots), 0) == along - along // cap * cap))
    cluster_row = jnp.sum(
        jnp.where(iota((n, slots), 0) == iota((n, slots), 1) // cap, wide, 0.0), axis=0, keepdims=True
    )
    whole(EMB).wait_recv()
    scale = 2.0 / math.sqrt(emb_ref.shape[1])
    for offset in range(0, slots, chunk):
        score = dot_nt(recv_emb[pl.ds(offset, chunk), :], recv_emb[...]) * scale
        score = jnp.where(cluster_col[offset : offset + chunk] != cluster_row, score - cross_penalty, score)
        score = jnp.where(cluster_row > 0.5, score, -1e30)
        score = jnp.where(iota(score.shape, 0) + offset == iota(score.shape, 1), 0.0, score)
        weight = jnp.exp(score - jnp.max(score, axis=1, keepdims=True))
        total = jnp.sum(weight, axis=1, keepdims=True)
        affinity[pl.ds(offset, chunk), :] = (weight * (1.0 / total)).astype(jnp.bfloat16)

    whole(LABEL).wait_recv()
    given = recv_lab[...].astype(jnp.float32)
    fixed = seed_col > 0.5
    carried[...] = recv_lab[...]
    for sweep in range(STEPS - 1):
        spread = dot(affinity[...], carried[...])
        current = jnp.where(fixed, given, label_mix * spread + (1.0 - label_mix) * given)
        carried[...] = current.astype(jnp.bfloat16)

    for j in range(1, n_grp + 1):
        g = lax.rem(my_grp + j, n_grp)
        piece = pl.ds(pl.multiple_of(g * chunk, chunk), chunk)
        send_back[piece, :] = dot(affinity[piece, :], carried[...]).astype(jnp.bfloat16)
        members_of(j, lambda d: copy(BACK, d, me).start())
    recv_back[block(me), :] = send_back[block(me), :]

    whole(BACK).wait_recv()
    spread = dot(home[...], recv_back[...])
    seed = lab_ref[...]
    out_ref[...] = jnp.where(kept, seed, label_mix * spread + (1.0 - label_mix) * seed)

    for kind in (EMB, LABEL, INFO, BACK):
        whole(kind).wait_send()


def solution(mesh):
    n_grp, n_peer = mesh.shape["grp"], mesh.shape["peer"]
    n = n_grp * n_peer

    def step(embeddings, seed_labels, cluster_ids, owner_map, seed_flags):
        rows, depth = embeddings.shape
        width = seed_labels.shape[1]
        cap = max(2 * rows // n, 16)
        slots = n * cap
        buffers = [
            pltpu.VMEM((slots, depth), jnp.bfloat16),
            pltpu.VMEM((slots, width), jnp.bfloat16),
            pltpu.VMEM((n, 1, 128), jnp.float32),
        ]
        return pl.pallas_call(
            functools.partial(kernel, n_grp, n_peer, cap),
            out_shape=jax.ShapeDtypeStruct((rows, width), jnp.float32),
            in_specs=[pl.BlockSpec(memory_space=pltpu.VMEM)] * 5,
            out_specs=pl.BlockSpec(memory_space=pltpu.VMEM),
            scratch_shapes=[
                *buffers,
                *buffers,
                pltpu.VMEM((slots, width), jnp.bfloat16),
                pltpu.VMEM((slots, width), jnp.bfloat16),
                pltpu.VMEM((1, rows), jnp.int32),
                pltpu.VMEM((rows, slots), jnp.bfloat16),
                pltpu.VMEM((slots, slots), jnp.bfloat16),
                pltpu.VMEM((slots, width), jnp.bfloat16),
                pltpu.SemaphoreType.DMA((4,)),
                pltpu.SemaphoreType.DMA((4,)),
            ],
            compiler_params=pltpu.CompilerParams(
                collective_id=0, has_side_effects=True, vmem_limit_bytes=56 * 1024 * 1024
            ),
        )(embeddings, seed_labels, cluster_ids, owner_map, seed_flags)

    rows = P(("grp", "peer"))
    return jax.shard_map(
        step,
        mesh=mesh,
        in_specs=(P(("grp", "peer"), None), P(("grp", "peer"), None), rows, P(), rows),
        out_specs=P(("grp", "peer"), None),
        check_vma=False,
    )
```
